256 devices in a mesh: dp: 16 (over z, x_hi), expert: 16 (over y, x_lo, core).
Axes of the slice: x: 4 (x_hi: 2, x_lo: 2; x = x_hi * 2 + x_lo), y: 4, z: 8, core: 2. Of those that a mesh axis runs over, the one named last changes fastest.
Arguments:
- tokens: bfloat16 [65536, 1024], P(('dp', 'expert')), may hold values from -24 to 24
- expert_ids: int32 [65536, 2], P(('dp', 'expert')), may hold values from 0 to 31, all different within a row; in each aligned block of 256 rows (0 to 255, 256 to 511, ...) at most 40 rows name the same one
- gate_quant: int32 [65536], P(('dp', 'expert')), may hold values from 1 to 255
- cotangent: bfloat16 [65536, 1024], P(('dp', 'expert')), may hold values from -3 to 3
- w_gate: bfloat16 [32, 1024, 512], P('expert'), may hold values from -0.1875 to 0.1875
- w_up: bfloat16 [32, 1024, 512], P('expert'), may hold values from -0.1875 to 0.1875
- w_down: bfloat16 [32, 512, 1024], P('expert'), may hold values from -0.25 to 0.25
Outputs:
- layer_out: bfloat16 [65536, 1024], P(('dp', 'expert'))
- grad_tokens: bfloat16 [65536, 1024], P(('dp', 'expert'))
- grad_w_gate: float32 [32, 1024, 512], P('expert', 'dp')
- grad_w_up: float32 [32, 1024, 512], P('expert', 'dp')
- grad_w_down: float32 [32, 512, 1024], P('expert', 'dp')
The draws below stay inside these ranges and needn't reach their ends.
Inputs may be any that keep to these rules, and one draw needn't show every extreme that they name: `expert_ids`: each row names two different experts. Within the 256 rows of one device no expert is named more than 40 times, and in every draw some device names some expert exactly 40 times.
All inputs are finite; a program needn't handle non-finite values.
Results may differ from the reference program's by a relative error of at most 0.017.
Values may be sent and summed in bfloat16 or wider, within the bound.
No kernel may reach another device: no remote copies, remote signals or barrier semaphores. Data moves between devices by JAX's collectives and lax.ppermute only.
A program may use at most 128 MiB of HBM per device.

```python
import math
import jax
import jax.numpy as jnp
import numpy as np
from jax import lax

D = 1024
HID = 512
EXPERTS = 32
TOK_DEV = 256
CAP = 40
TOKENS = 65536
N_DP = 16
N_EXPERT = 16


def with_ends(drawn, key, least, top_value):
    index_at = [jax.random.randint(jax.random.fold_in(key, axis), (), 0, length) for axis, length in enumerate(drawn.shape)]
    widest = drawn.shape.index(max(drawn.shape))
    beside = index_at[:widest] + [(index_at[widest] + 1) % drawn.shape[widest]] + index_at[widest + 1:]
    return drawn.at[tuple(index_at)].set(least).at[tuple(beside)].set(top_value)


def raised(array, key, source, target, shards_of, factor):
    def block_of(dim):
        return (jnp.arange(array.shape[dim]) // (array.shape[dim] // shards_of)).reshape((-1,) + (1,) * (array.ndim - 1 - dim))

    one_side = jax.random.permutation(key, shards_of)[block_of(target)]
    far = (block_of(target) + shards_of // 2) % shards_of
    return jnp.where((block_of(source) == one_side) | (block_of(source) == far), factor * array, array)


def steps_of(own_key, shape, cuts, smallest, high):
    def one(axis_at, shards_of):
        heights = jax.random.uniform(jax.random.fold_in(jax.random.fold_in(own_key, 6), axis_at), (shards_of,), jnp.float32, smallest / len(cuts), high / len(cuts))
        return jnp.repeat(jnp.exp(heights), shape[axis_at] // shards_of).reshape((-1,) + (1,) * (len(shape) - axis_at - 1))

    level = one(*cuts[0])
    for cut in cuts[1:]:
        level = level * one(*cut)
    return level


def routed_block(own_key, own, number, rows, count, top, bound, lean):
    sequence = jax.random.permutation(own_key, count)
    crowded, usual = portions_of(count, rows * top, bound, lean, True), portions_of(count, rows * top, bound, lean, False)
    places = jnp.arange(count)

    def named(tallies, turn):
        used = int((tallies > 0).sum())
        fixed = max(1, used // 4)
        moved = fixed + (places - fixed + turn * (used - fixed)) % max(1, count - fixed)
        return jnp.zeros((count,), jnp.int32).at[sequence[jnp.where(places < fixed, places, moved)]].set(jnp.asarray(tallies, jnp.int32))

    tallies = jnp.where(number % 4 == 0, named(crowded, number // 4), named(usual, number - number // 4 - 1))
    mixed = jax.random.permutation(jax.random.fold_in(own, 3), count)
    giver, taker = mixed[0:count // 2 * 2:2], mixed[1:count // 2 * 2:2]
    room = jnp.minimum(tallies[giver] - 1, bound - tallies[taker]) // 2
    room = jnp.where((giver == sequence[0]) | (taker == sequence[0]) | (tallies[taker] == 0), 0, jnp.maximum(room, 0))
    moved = jax.random.randint(jax.random.fold_in(own, 4), (count // 2,), 0, 1 << 20) % (room + 1)
    tallies = tallies.at[giver].add(-moved).at[taker].add(moved)
    labels = jnp.searchsorted(jnp.cumsum(tallies), jnp.arange(rows * top), side="right").astype(jnp.int32)
    table = labels.reshape(top, rows).T
    table = table[jax.random.permutation(jax.random.fold_in(own, 1), rows)]
    turn = jax.random.randint(jax.random.fold_in(own, 2), (rows, 1), 0, top)
    return jnp.take_along_axis(table, (jnp.arange(top)[None, :] + turn) % top, axis=1)


def portions_of(count, total, limit, lean, full):
    weights = [(1 << 20) // math.isqrt(standing ** lean) + 1 for standing in range(1, count + 1)]
    largest = limit if full else min(limit, max(-(-total // count), total * weights[0] // sum(weights)))
    least = 1 if total - largest >= count - 1 else 0
    holding, spare = [largest] + [least] * (count - 1), total - largest - least * (count - 1)
    while spare > 0:
        free = [i for i in range(1, count) if holding[i] < largest] or [i for i in range(1, count) if holding[i] < limit]
        whole, remaining = sum([weights[i] for i in free]), spare
        for i in free:
            addition = min(limit - holding[i], max(1, remaining * weights[i] // whole), spare)
            holding[i] = holding[i] + addition
            spare = spare - addition
    return np.array(holding)


def scatter_about(own_key, dims, width, bound, split=(), held_as=jnp.bfloat16):
    values = jax.random.normal(own_key, dims, jnp.float32) * width
    if len(split) > 0:
        values = steps_of(own_key, dims, split, -0.22, 0.18) * values
    return jnp.clip(values, min=-bound, max=bound).astype(held_as)


def noise_with(rng, dims, spread, limit, pieces, heavy, held_as=jnp.bfloat16):
    array = spread * jax.random.normal(rng, dims, jnp.float32)
    if pieces:
        array = array * steps_of(rng, dims, pieces, -0.22, 0.18)
    return jnp.clip(raised(array, jax.random.fold_in(rng, 3), *heavy), -limit, limit).astype(held_as)


def setup_inputs(seed: int = 0) -> dict:
    key_of = jax.random.split(jax.random.key(seed), 8)
    tokens = noise_with(key_of[0], (TOKENS, D), 1.0, 24.0, ((0, 256),), (0, 1, 256, 6.0))
    expert_ids_keys = jax.random.split(jax.random.fold_in(key_of[1], 1), TOKENS // TOK_DEV)
    expert_ids_turns = jax.random.permutation(jax.random.fold_in(key_of[1], 3), TOKENS // TOK_DEV)
    expert_ids = jax.vmap(lambda own, number: routed_block(jax.random.fold_in(key_of[1], 2), own, number, TOK_DEV, EXPERTS, 2, CAP, 2))(expert_ids_keys, expert_ids_turns).reshape((TOKENS, 2))
    gate_quant = with_ends(jax.random.randint(key_of[2], (TOKENS,), 1, 256), jax.random.fold_in(key_of[2], 1), 1, 255).astype(jnp.int32)
    cotangent = scatter_about(key_of[3], (TOKENS, D), 0.5, 3.0, ((0, 256),))
    w_gate = scatter_about(key_of[4], (EXPERTS, D, HID), D ** -0.5, 0.1875, ((0, 16),))
    w_up = scatter_about(key_of[5], (EXPERTS, D, HID), D ** -0.5, 0.1875, ((0, 16),))
    w_down = scatter_about(key_of[6], (EXPERTS, HID, D), HID ** -0.5, 0.25, ((0, 16),))
    return dict(tokens=tokens, expert_ids=expert_ids, gate_quant=gate_quant, cotangent=cotangent, w_gate=w_gate, w_up=w_up, w_down=w_down)


def slot_places(expert_ids):
    flat_ids = expert_ids.reshape(-1)
    choose = (flat_ids[:, None] == jnp.arange(EXPERTS, dtype=jnp.int32)[None, :]).astype(jnp.int32)
    earlier = jnp.cumsum(choose, axis=0) - choose
    return (flat_ids * CAP + jnp.sum(earlier * choose, axis=1)).astype(jnp.int32)


def place_rows(slot_index, values):
    blank_rows = jnp.zeros((EXPERTS * CAP, values.shape[1]), values.dtype)
    return blank_rows.at[slot_index].set(values)


def by_expert(sent):
    return sent.reshape(N_EXPERT, EXPERTS, CAP, D).transpose(1, 0, 2, 3).reshape(EXPERTS, N_EXPERT * CAP, D)


def from_expert(result):
    return result.reshape(EXPERTS, N_EXPERT, CAP, D).transpose(1, 0, 2, 3).reshape(N_EXPERT, EXPERTS * CAP, D)


def expert_pass(operands):
    token_rows, routed_rows, gate_weight, up_weight, down_weight = operands
    gate_value = jnp.dot(token_rows, gate_weight, preferred_element_type=jnp.float32)
    up_value = jnp.dot(token_rows, up_weight, preferred_element_type=jnp.float32)
    sigmoid_gate = jax.nn.sigmoid(gate_value)
    activated = gate_value * sigmoid_gate
    hidden = (activated * up_value).astype(jnp.bfloat16)
    expert_out = jnp.dot(hidden, down_weight, preferred_element_type=jnp.float32).astype(jnp.bfloat16)
    hidden_grad = jnp.dot(routed_rows, down_weight.T, preferred_element_type=jnp.float32)
    gate_grad = (hidden_grad * up_value * sigmoid_gate * (1.0 + gate_value * (1.0 - sigmoid_gate))).astype(jnp.bfloat16)
    up_grad = (hidden_grad * activated).astype(jnp.bfloat16)
    input_grad = (jnp.dot(gate_grad, gate_weight.T, preferred_element_type=jnp.float32)
                  + jnp.dot(up_grad, up_weight.T, preferred_element_type=jnp.float32)).astype(jnp.bfloat16)
    part_gate = jnp.dot(token_rows.T, gate_grad, preferred_element_type=jnp.float32).astype(jnp.bfloat16)
    part_up = jnp.dot(token_rows.T, up_grad, preferred_element_type=jnp.float32).astype(jnp.bfloat16)
    part_down = jnp.dot(hidden.T, routed_rows, preferred_element_type=jnp.float32).astype(jnp.bfloat16)
    return expert_out, input_grad, part_gate, part_up, part_down


def pick_rows(rows_back, places):
    return rows_back[places]


def reference(tokens, expert_ids, gate_quant, cotangent, w_gate, w_up, w_down):
    def group_pass(totals, group_data):
        group_tokens, group_ids, group_quant, group_cot = group_data
        slot_index = jax.vmap(slot_places)(group_ids)
        first_share = group_quant.astype(jnp.float32) / 256.0
        shares = jnp.stack([first_share, 1.0 - first_share], axis=2)
        doubled = jnp.repeat(group_tokens, 2, axis=1)
        routed = (shares[:, :, :, None] * group_cot[:, :, None, :].astype(jnp.float32)).astype(jnp.bfloat16)
        routed = routed.reshape(N_EXPERT, 2 * TOK_DEV, D)
        sent_tokens = jax.vmap(place_rows)(slot_index, doubled)
        sent_grads = jax.vmap(place_rows)(slot_index, routed)
        expert_out, input_grad, part_gate, part_up, part_down = lax.map(
            expert_pass, (by_expert(sent_tokens), by_expert(sent_grads), w_gate, w_up, w_down))
        picked = jax.vmap(pick_rows)(from_expert(expert_out), slot_index)
        picked = picked.reshape(N_EXPERT, TOK_DEV, 2, D).astype(jnp.float32)
        layer_out = jnp.sum(shares[:, :, :, None] * picked, axis=2).astype(jnp.bfloat16)
        picked_grad = jax.vmap(pick_rows)(from_expert(input_grad), slot_index)
        picked_grad = picked_grad.reshape(N_EXPERT, TOK_DEV, 2, D).astype(jnp.float32)
        grad_tokens = (picked_grad[:, :, 0] + picked_grad[:, :, 1]).astype(jnp.bfloat16)
        totals = (totals[0] + part_gate.astype(jnp.float32),
                  totals[1] + part_up.astype(jnp.float32),
                  totals[2] + part_down.astype(jnp.float32))
        return totals, (layer_out, grad_tokens)

    initial = (jnp.zeros((EXPERTS, D, HID), jnp.float32),
               jnp.zeros((EXPERTS, D, HID), jnp.float32),
               jnp.zeros((EXPERTS, HID, D), jnp.float32))
    inputs = (tokens.reshape(N_DP, N_EXPERT, TOK_DEV, D),
              expert_ids.reshape(N_DP, N_EXPERT, TOK_DEV, 2),
              gate_quant.reshape(N_DP, N_EXPERT, TOK_DEV),
              cotangent.reshape(N_DP, N_EXPERT, TOK_DEV, D))
    totals, stacked = lax.scan(group_pass, initial, inputs)
    layer_out = stacked[0].reshape(TOKENS, D)
    grad_tokens = stacked[1].reshape(TOKENS, D)
    return (layer_out, grad_tokens, totals[0], totals[1], totals[2])
```

```python
import jax
import jax.numpy as jnp
from jax import lax
from jax.experimental import pallas as pl
from jax.experimental.pallas import tpu as pltpu
from jax.sharding import PartitionSpec as P

D = 1024
HID = 512
TOK = 256
CAP = 40
GROUPS = 16
CHUNKS = 2
ROWS = GROUPS * CAP
RING = 8
HI = 2
GATE_ROWS = D // RING // HI
DOWN_ROWS = HID // RING // HI
SHARD_ROWS = GATE_ROWS + DOWN_ROWS
VMEM = pl.BlockSpec(memory_space=pltpu.VMEM)
SMEM = pl.BlockSpec(memory_space=pltpu.SMEM)
BF16 = jnp.bfloat16
F32 = jnp.float32


def mm(a, b, dims=((1,), (0,))):
    return lax.dot_general(a, b, (dims, ((), ())), preferred_element_type=F32)


def slot_rows(ids_ref, quant_ref, chunk):
    first, second = ids_ref[0:1, :], ids_ref[1:2, :]
    expert = lax.broadcasted_iota(jnp.int32, (GROUPS, TOK), 0) * CHUNKS + chunk
    is_first = expert == first
    chosen = is_first | (expert == second)
    before = lax.broadcasted_iota(jnp.int32, (TOK, TOK), 0) < lax.broadcasted_iota(
        jnp.int32, (TOK, TOK), 1
    )
    rank = mm(
        jnp.where(chosen, 1.0, 0.0).astype(BF16), jnp.where(before, 1.0, 0.0).astype(BF16)
    )
    place = jnp.where(chosen, rank.astype(jnp.int32), -1)
    share = quant_ref[...].astype(F32) / 256.0
    share = jnp.where(is_first, share, 1.0 - share)
    row = lax.broadcasted_iota(jnp.int32, (CAP, TOK), 0)
    hit = [row == place[g : g + 1, :] for g in range(GROUPS)]
    plain = jnp.concatenate([jnp.where(h, 1.0, 0.0) for h in hit], axis=0)
    weighted = jnp.concatenate(
        [jnp.where(h, share[g : g + 1, :], 0.0) for g, h in enumerate(hit)], axis=0
    )
    return plain.astype(BF16), weighted.astype(BF16)


def pack_kernel(ids_ref, quant_ref, tokens_ref, cot_ref, *send_refs):
    for chunk, send_ref in enumerate(send_refs):
        plain, weighted = slot_rows(ids_ref, quant_ref, chunk)
        send_ref[:, 0] = mm(plain, tokens_ref[...]).reshape(GROUPS, CAP, D).astype(BF16)
        send_ref[:, 1] = mm(weighted, cot_ref[...]).reshape(GROUPS, CAP, D).astype(BF16)


def pack(ids, quant, tokens, cotangent):
    shape = jax.ShapeDtypeStruct((GROUPS, 2, CAP, D), BF16)
    return pl.pallas_call(
        pack_kernel,
        out_shape=[shape] * CHUNKS,
        in_specs=[VMEM] * 4,
        out_specs=[VMEM] * CHUNKS,
        compiler_params=pltpu.CompilerParams(vmem_limit_bytes=40 << 20),
        cost_estimate=pl.CostEstimate(
            flops=4 * CHUNKS * ROWS * TOK * D, bytes_accessed=7 << 20, transcendentals=0
        ),
        name="pack",
    )(ids, quant, tokens, cotangent)


def expert_kernel(z_ref, recv_ref, gate_ref, up_ref, down_ref, ret_ref, *refs):
    part_refs, (grad_gu, grad_down) = refs[:RING], refs[RING:]
    rows = recv_ref[:, 0].astype(F32).reshape(ROWS, D).astype(BF16)
    routed = recv_ref[:, 1].astype(F32).reshape(ROWS, D).astype(BF16)
    w_gate, w_up, w_down = gate_ref[0], up_ref[0], down_ref[0]
    gate_value = mm(rows, w_gate)
    up_value = mm(rows, w_up)
    sig = jax.nn.sigmoid(gate_value)
    act = gate_value * sig
    hidden = (act * up_value).astype(BF16)
    hidden_grad = mm(routed, w_down, ((1,), (1,)))
    gate_grad = (hidden_grad * up_value * sig * (1.0 + gate_value * (1.0 - sig))).astype(BF16)
    up_grad = (hidden_grad * act).astype(BF16)
    both = jnp.concatenate([gate_grad, up_grad], axis=1)
    grad_gu[...] = mm(rows, both, ((0,), (0,)))
    grad_down[...] = mm(hidden, routed, ((0,), (0,)))
    z = z_ref[0]
    for j, part_ref in enumerate(part_refs):
        owner = lax.rem(z + j, RING)
        for h in range(HI):
            at = pl.multiple_of((owner * HI + h) * GATE_ROWS, GATE_ROWS)
            part_ref[h, :GATE_ROWS] = grad_gu[pl.ds(at, GATE_ROWS), :].astype(BF16)
            at = pl.multiple_of((owner * HI + h) * DOWN_ROWS, DOWN_ROWS)
            part_ref[h, GATE_ROWS:] = grad_down[pl.ds(at, DOWN_ROWS), :].astype(BF16)
    ret_ref[:, 0] = mm(hidden, w_down).reshape(GROUPS, CAP, D).astype(BF16)
    input_grad = mm(gate_grad, w_gate, ((1,), (1,))) + mm(up_grad, w_up, ((1,), (1,)))
    ret_ref[:, 1] = input_grad.reshape(GROUPS, CAP, D).astype(BF16)


def expert(z, recv, w_gate, w_up, w_down, chunk):
    part = jax.ShapeDtypeStruct((HI, SHARD_ROWS, D), BF16)

    def whole(*shape):
        return pl.BlockSpec(shape, lambda i: (0,) * len(shape))

    def one(*shape):
        return pl.BlockSpec((1,) + shape, lambda i: (chunk, 0, 0))

    out = pl.pallas_call(
        expert_kernel,
        grid=(1,),
        out_shape=[jax.ShapeDtypeStruct((GROUPS, 2, CAP, D), BF16)] + [part] * RING,
        in_specs=[
            SMEM,
            whole(GROUPS, 2, CAP, D),
            one(D, HID),
            one(D, HID),
            one(HID, D),
        ],
        out_specs=[whole(GROUPS, 2, CAP, D)] + [whole(HI, SHARD_ROWS, D)] * RING,
        scratch_shapes=[pltpu.VMEM((D, 2 * HID), F32), pltpu.VMEM((HID, D), F32)],
        compiler_params=pltpu.CompilerParams(vmem_limit_bytes=56 << 20),
        cost_estimate=pl.CostEstimate(
            flops=18 * ROWS * D * HID, bytes_accessed=12 << 20, transcendentals=ROWS * HID
        ),
        name=f"expert_{chunk}",
    )(z, recv, w_gate, w_up, w_down)
    return out[0], out[1:]


def unpack_kernel(ids_ref, quant_ref, *refs):
    ret_refs, (layer_ref, grad_ref) = refs[:CHUNKS], refs[CHUNKS:]
    layer, grad = 0.0, 0.0
    for chunk, ret_ref in enumerate(ret_refs):
        plain, weighted = slot_rows(ids_ref, quant_ref, chunk)
        outs = ret_ref[:, 0].astype(F32).reshape(ROWS, D).astype(BF16)
        layer += mm(weighted, outs, ((0,), (0,)))
        grads = ret_ref[:, 1].astype(F32).reshape(ROWS, D).astype(BF16)
        grad += mm(plain, grads, ((0,), (0,)))
    layer_ref[...] = layer.astype(BF16)
    grad_ref[...] = grad.astype(BF16)


def unpack(ids, quant, returned):
    shape = jax.ShapeDtypeStruct((TOK, D), BF16)
    return pl.pallas_call(
        unpack_kernel,
        out_shape=[shape] * 2,
        in_specs=[VMEM] * (2 + CHUNKS),
        out_specs=[VMEM] * 2,
        compiler_params=pltpu.CompilerParams(vmem_limit_bytes=40 << 20),
        cost_estimate=pl.CostEstimate(
            flops=4 * CHUNKS * ROWS * TOK * D, bytes_accessed=7 << 20, transcendentals=0
        ),
        name="unpack",
    )(ids, quant, *returned)


def chain(parts, hops, sign):
    step = [(i, (i // HI + sign) % RING * HI + i % HI) for i in range(RING * HI)]
    held = parts[sign * hops % RING]
    for j in range(hops - 1, -1, -1):
        held = lax.ppermute(held, "dp", step)
        if j:
            held = (held.astype(F32) + parts[sign * j % RING].astype(F32)).astype(BF16)
    return held


def reduce_shards(parts, up_hops):
    arrived_up = chain(parts, up_hops, 1)
    arrived_down = chain(parts, RING - 1 - up_hops, -1)
    total = parts[0].astype(F32) + arrived_up.astype(F32) + arrived_down.astype(F32)
    hi = lax.axis_index("dp") % HI
    mine = lax.dynamic_index_in_dim(total, hi, 0, keepdims=False)
    other = lax.dynamic_index_in_dim(total, 1 - hi, 0, keepdims=False).astype(BF16)
    got = lax.ppermute(other, "dp", [(i, i ^ 1) for i in range(RING * HI)])
    return mine + got.astype(F32)


def per_device(tokens, expert_ids, gate_quant, cotangent, w_gate, w_up, w_down):
    ids, quant = expert_ids.T, gate_quant[None, :]
    z = (lax.axis_index("dp") // HI).astype(jnp.int32).reshape(1)
    sends = pack(ids, quant, tokens, cotangent)
    returned, shards = [], []
    for chunk, send in enumerate(sends):
        recv = lax.all_to_all(send, "expert", 0, 0, tiled=True)
        ret, parts = expert(z, recv, w_gate, w_up, w_down, chunk)
        returned.append(lax.all_to_all(ret, "expert", 0, 0, tiled=True))
        shards.append(reduce_shards(parts, 3 + chunk))
    layer_out, grad_tokens = unpack(ids, quant, returned)
    shards = jnp.stack(shards)
    return (
        layer_out,
        grad_tokens,
        shards[:, :GATE_ROWS, :HID],
        shards[:, :GATE_ROWS, HID:],
        shards[:, GATE_ROWS:, :],
    )


def solution(mesh):
    return jax.shard_map(
        per_device,
        mesh=mesh,
        in_specs=(
            P(("dp", "expert"), None),
            P(("dp", "expert"), None),
            P(("dp", "expert")),
            P(("dp", "expert"), None),
            P("expert", None, None),
            P("expert", None, None),
            P("expert", None, None),
        ),
        out_specs=(
            P(("dp", "expert"), None),
            P(("dp", "expert"), None),
            P("expert", "dp", None),
            P("expert", "dp", None),
            P("expert", "dp", None),
        ),
        check_vma=False,
    )
```

```python
import functools

import jax
import jax.numpy as jnp
from jax import lax
from jax.experimental import pallas as pl
from jax.experimental.pallas import tpu as pltpu
from jax.sharding import PartitionSpec as P

D = 1024
HID = 512
TOK = 256
CAP = 40
GROUPS = 16
CHUNKS = 2
ROWS = GROUPS * CAP
RING = 8
HI = 2
GATE_ROWS = D // RING // HI
DOWN_ROWS = HID // RING // HI
SHARD_ROWS = GATE_ROWS + DOWN_ROWS
VMEM = pl.BlockSpec(memory_space=pltpu.VMEM)
ANY = pl.BlockSpec(memory_space=pl.ANY)
SMEM = pl.BlockSpec(memory_space=pltpu.SMEM)
BF16 = jnp.bfloat16
F32 = jnp.float32


def mm(a, b, dims=((1,), (0,))):
    return lax.dot_general(a, b, (dims, ((), ())), preferred_element_type=F32)


def whole(*shape):
    return pl.BlockSpec(shape, lambda i: (0,) * len(shape))


def one(chunk, *shape):
    return pl.BlockSpec((1,) + shape, lambda i: (chunk, 0, 0))


def slot_rows(ids_ref, quant_ref, chunk):
    first, second = ids_ref[0:1, :], ids_ref[1:2, :]
    expert = lax.broadcasted_iota(jnp.int32, (GROUPS, TOK), 0) * CHUNKS + chunk
    is_first = expert == first
    chosen = is_first | (expert == second)
    before = lax.broadcasted_iota(jnp.int32, (TOK, TOK), 0) < lax.broadcasted_iota(
        jnp.int32, (TOK, TOK), 1
    )
    rank = mm(
        jnp.where(chosen, 1.0, 0.0).astype(BF16), jnp.where(before, 1.0, 0.0).astype(BF16)
    )
    place = jnp.where(chosen, rank.astype(jnp.int32), -1)
    share = quant_ref[...].astype(F32) / 256.0
    share = jnp.where(is_first, share, 1.0 - share)
    row = lax.broadcasted_iota(jnp.int32, (CAP, TOK), 0)
    hit = [row == place[g : g + 1, :] for g in range(GROUPS)]
    plain = jnp.concatenate([jnp.where(h, 1.0, 0.0) for h in hit], axis=0)
    weighted = jnp.concatenate(
        [jnp.where(h, share[g : g + 1, :], 0.0) for g, h in enumerate(hit)], axis=0
    )
    return plain.astype(BF16), weighted.astype(BF16)


def pack_kernel(chunk, ids_ref, quant_ref, tokens_ref, cot_ref, *refs):
    send_ref, plain_ref, weighted_ref = refs[-3:]

    @pl.when(pl.program_id(0) == 0)
    def _():
        plain_ref[...], weighted_ref[...] = slot_rows(ids_ref, quant_ref, chunk)

    width = tokens_ref.shape[1]
    rows = mm(plain_ref[...], tokens_ref[...])
    send_ref[:, 0] = rows.reshape(GROUPS, CAP, width).astype(BF16)
    rows = mm(weighted_ref[...], cot_ref[...])
    send_ref[:, 1] = rows.reshape(GROUPS, CAP, width).astype(BF16)


def pack(ids, quant, tokens, cotangent, chunk, after):
    steps = 4
    columns = pl.BlockSpec((TOK, D // steps), lambda i: (0, i))
    return pl.pallas_call(
        functools.partial(pack_kernel, chunk),
        grid=(steps,),
        out_shape=pltpu.HBM((GROUPS, 2, CAP, D), BF16),
        in_specs=[whole(2, TOK), whole(1, TOK), columns, columns] + [ANY] * len(after),
        out_specs=pl.BlockSpec((GROUPS, 2, CAP, D // steps), lambda i: (0, 0, 0, i)),
        scratch_shapes=[pltpu.VMEM((ROWS, TOK), BF16)] * 2,
        compiler_params=pltpu.CompilerParams(vmem_limit_bytes=(60 if chunk == 0 else 24) << 20),
        cost_estimate=pl.CostEstimate(
            flops=4 * ROWS * TOK * D, bytes_accessed=4 << 20, transcendentals=0
        ),
        name=f"pack_{chunk}",
    )(ids, quant, tokens, cotangent, *after)


def pick_kernel(ids_ref, quant_ref, *pick_refs):
    for chunk, pick_ref in enumerate(pick_refs):
        for kind, rows in enumerate(slot_rows(ids_ref, quant_ref, chunk)):
            pick_ref[kind] = rows.astype(F32).T.astype(BF16)


def picks(ids, quant):
    return pl.pallas_call(
        pick_kernel,
        grid=(1,),
        out_shape=[pltpu.HBM((2, TOK, ROWS), BF16)] * CHUNKS,
        in_specs=[whole(2, TOK), whole(1, TOK)],
        out_specs=[whole(2, TOK, ROWS)] * CHUNKS,
        compiler_params=pltpu.CompilerParams(vmem_limit_bytes=20 << 20),
        cost_estimate=pl.CostEstimate(
            flops=4 * TOK * TOK * GROUPS, bytes_accessed=2 << 20, transcendentals=0
        ),
        name="picks",
    )(ids, quant)


def expert_kernel(chunk, waits, z_ref, recv_ref, gate_ref, up_ref, down_ref, *refs):
    hidden_ref, grads_ref, *refs = refs[waits:]
    part_refs, (grad_gu, grad_down, *held, sems) = refs[:RING], refs[RING:]
    recv, w_gate, w_up, w_down = held
    sources = (recv_ref, gate_ref.at[chunk], up_ref.at[chunk], down_ref.at[chunk])
    loads = [
        pltpu.make_async_copy(source, to, sems.at[i])
        for i, (source, to) in enumerate(zip(sources, held))
    ]
    for load in loads:
        load.start()
    loads[0].wait()
    rows = recv[:, 0].astype(F32).reshape(ROWS, D).astype(BF16)
    routed = recv[:, 1].astype(F32).reshape(ROWS, D).astype(BF16)
    loads[1].wait()
    gate_value = mm(rows, w_gate[...])
    loads[2].wait()
    up_value = mm(rows, w_up[...])
    sig = jax.nn.sigmoid(gate_value)
    act = gate_value * sig
    hidden = (act * up_value).astype(BF16)
    loads[3].wait()
    hidden_grad = mm(routed, w_down[...], ((1,), (1,)))
    gate_grad = (hidden_grad * up_value * sig * (1.0 + gate_value * (1.0 - sig))).astype(BF16)
    up_grad = (hidden_grad * act).astype(BF16)
    both = jnp.concatenate([gate_grad, up_grad], axis=1)
    hidden_ref[...] = hidden
    grads_ref[...] = both
    grad_gu[...] = mm(rows, both, ((0,), (0,)))
    grad_down[...] = mm(hidden, routed, ((0,), (0,)))
    z = z_ref[0]
    for j, part_ref in enumerate(part_refs):
        owner = lax.rem(z + j, RING)
        for h in range(HI):
            at = pl.multiple_of((owner * HI + h) * GATE_ROWS, GATE_ROWS)
            part_ref[h, :GATE_ROWS] = grad_gu[pl.ds(at, GATE_ROWS), :].astype(BF16)
            at = pl.multiple_of((owner * HI + h) * DOWN_ROWS, DOWN_ROWS)
            part_ref[h, GATE_ROWS:] = grad_down[pl.ds(at, DOWN_ROWS), :].astype(BF16)


def held_in(space, *arrays):
    return [pltpu.with_memory_space_constraint(a, space) for a in arrays]


def expert(z, recv, w_gate, w_up, w_down, chunk, after):
    part = pltpu.VMEM((HI, SHARD_ROWS, D), BF16)
    weight = 3 if chunk else 1
    hidden, grads, *parts = pl.pallas_call(
        functools.partial(expert_kernel, chunk, len(after)),
        out_shape=[pltpu.VMEM((ROWS, HID), BF16), pltpu.VMEM((ROWS, 2 * HID), BF16)]
        + [part] * RING,
        in_specs=[SMEM] + [ANY] * (4 + len(after)),
        out_specs=[VMEM] * (2 + RING),
        scratch_shapes=[pltpu.VMEM((D, 2 * HID), F32), pltpu.VMEM((HID, D), F32)]
        + [pltpu.VMEM((GROUPS, 2, CAP, D), BF16)]
        + [pltpu.VMEM((D, HID), BF16)] * 2
        + [pltpu.VMEM((HID, D), BF16), pltpu.SemaphoreType.DMA((4,))],
        compiler_params=pltpu.CompilerParams(vmem_limit_bytes=27 << 20),
        cost_estimate=pl.CostEstimate(
            flops=weight * 12 * ROWS * D * HID,
            bytes_accessed=weight * 10 << 20,
            transcendentals=ROWS * HID,
        ),
        name=f"expert_{chunk}",
    )(z, *held_in(pltpu.HBM, recv, w_gate, w_up, w_down), *after)
    return hidden, grads, parts


def answer_kernel(hidden_ref, grads_ref, gate_ref, up_ref, down_ref, *refs):
    ret_ref = refs[-1]
    groups = ret_ref.shape[0]
    out = mm(hidden_ref[...], down_ref[0])
    ret_ref[:, 0] = out.reshape(groups, CAP, D).astype(BF16)
    input_grad = mm(grads_ref[:, :HID], gate_ref[0], ((1,), (1,)))
    input_grad += mm(grads_ref[:, HID:], up_ref[0], ((1,), (1,)))
    ret_ref[:, 1] = input_grad.reshape(groups, CAP, D).astype(BF16)


def answer(hidden, grads, w_gate, w_up, w_down, chunk, after):
    steps = 2
    return pl.pallas_call(
        answer_kernel,
        grid=(steps,),
        out_shape=pltpu.HBM((GROUPS, 2, CAP, D), BF16),
        in_specs=[
            pl.BlockSpec((ROWS // steps, HID), lambda i: (i, 0)),
            pl.BlockSpec((ROWS // steps, 2 * HID), lambda i: (i, 0)),
        ]
        + [one(chunk, D, HID), one(chunk, D, HID), one(chunk, HID, D)]
        + [ANY] * len(after),
        out_specs=pl.BlockSpec((GROUPS // steps, 2, CAP, D), lambda i: (i, 0, 0, 0)),
        compiler_params=pltpu.CompilerParams(vmem_limit_bytes=24 << 20),
        cost_estimate=pl.CostEstimate(
            flops=6 * ROWS * D * HID, bytes_accessed=8 << 20, transcendentals=0
        ),
        name=f"answer_{chunk}",
    )(hidden, grads, *held_in(pltpu.HBM, w_gate, w_up, w_down), *after)


def unpack_kernel(pick_ref, ret_ref, *refs):
    *earlier, layer_ref, grad_ref = refs
    width = layer_ref.shape[1]
    for kind, out_ref in ((0, layer_ref), (1, grad_ref)):
        rows = ret_ref[:, kind].astype(F32).reshape(ROWS, width).astype(BF16)
        total = mm(pick_ref[1 - kind], rows)
        if earlier:
            total += earlier[kind][...]
        out_ref[...] = total.astype(out_ref.dtype)


def unpack(pick, returned, chunk, earlier):
    steps = 2
    columns = pl.BlockSpec((TOK, D // steps), lambda i: (0, i))
    last = chunk == CHUNKS - 1
    return pl.pallas_call(
        unpack_kernel,
        grid=(steps,),
        out_shape=[jax.ShapeDtypeStruct((TOK, D), BF16 if last else F32)] * 2,
        in_specs=[
            whole(2, TOK, ROWS),
            pl.BlockSpec((GROUPS, 2, CAP, D // steps), lambda i: (0, 0, 0, i)),
        ]
        + [columns] * len(earlier),
        out_specs=[columns] * 2,
        compiler_params=pltpu.CompilerParams(vmem_limit_bytes=20 << 20),
        cost_estimate=pl.CostEstimate(
            flops=4 * ROWS * TOK * D, bytes_accessed=4 << 20, transcendentals=0
        ),
        name=f"unpack_{chunk}",
    )(*held_in(pltpu.HBM, pick, returned), *earlier)


def nothing(*refs):
    pass


def gate(array, *after):
    return pl.pallas_call(
        nothing,
        out_shape=pltpu.HBM(array.shape, array.dtype),
        in_specs=[ANY] * (1 + len(after)),
        out_specs=pl.BlockSpec(memory_space=pltpu.HBM),
        input_output_aliases={0: 0},
        cost_estimate=pl.CostEstimate(flops=0, bytes_accessed=0, transcendentals=0),
        name="gate",
    )(*held_in(pltpu.HBM, array), *after)


def ring_step(held, sign, across=0):
    step = [
        (i, (i // HI + sign) % RING * HI + (i + across) % HI) for i in range(RING * HI)
    ]
    return lax.ppermute(held, "dp", step)


def add_part(held, part):
    return (held.astype(F32) + part.astype(F32)).astype(BF16)


class Ring:
    def __init__(self, parts, up_hops):
        self.parts = parts
        self.hops = {1: up_hops, -1: RING - 1 - up_hops}
        self.held = {s: parts[s * n % RING] for s, n in self.hops.items()}

    def step(self, up=(), down=()):
        for sign, left in self.hops.items():
            if left:
                self.hops[sign] = left - 1
                held = ring_step(self.held[sign], sign)
                if left > 1:
                    part, *_ = lax.optimization_barrier(
                        (self.parts[sign * (left - 1) % RING], *(up if sign > 0 else down))
                    )
                    held = add_part(held, part)
                self.held[sign] = held

    def now(self):
        return self.held[1], self.held[-1]

    def before(self, *others):
        up, down, *others = lax.optimization_barrier((self.held[1], self.held[-1], *others))
        self.held = {1: up, -1: down}
        return others

    def finish(self):
        total = (
            self.parts[0].astype(F32) + self.held[1].astype(F32) + self.held[-1].astype(F32)
        )
        mine, other = halves(total)
        return mine + ring_step(other.astype(BF16), 0, 1).astype(F32)

    def finish_direct(self, sign):
        total = self.parts[0].astype(F32) + self.held[-sign].astype(F32)
        mine, other = halves(total)
        same, cross = halves(self.held[sign])
        arrived = [
            ring_step(same, sign),
            ring_step(cross, sign, 1),
            ring_step(other.astype(BF16), 0, 1),
        ]
        return mine + sum(a.astype(F32) for a in arrived)


def halves(pair):
    hi = lax.axis_index("dp") % HI
    return [lax.dynamic_index_in_dim(pair, h, 0, keepdims=False) for h in (hi, 1 - hi)]


def exchange(rows):
    return lax.all_to_all(rows, "expert", 0, 0, tiled=True)


def per_device(tokens, expert_ids, gate_quant, cotangent, w_gate, w_up, w_down):
    ids, quant = expert_ids.T, gate_quant[None, :]
    weights = (w_gate, w_up, w_down)
    z = (lax.axis_index("dp") // HI).astype(jnp.int32).reshape(1)
    pick = picks(ids, quant)
    recv_0 = exchange(pack(ids, quant, tokens, cotangent, 0, ()))
    recv_1 = exchange(pack(ids, quant, tokens, cotangent, 1, pick))
    hidden_0, grads_0, parts_0 = expert(z, recv_0, *weights, 0, ())
    ring_0 = Ring(parts_0, 3)
    ret_0 = answer(hidden_0, grads_0, *weights, 0, ())
    ring_0.step()
    back_0 = exchange(gate(ret_0, *ring_0.now()))
    ring_0.step()
    hidden_1, grads_1, parts_1 = expert(z, recv_1, *weights, 1, ring_0.now())
    ring_1 = Ring(parts_1, 4)
    ring_1.step()
    ret_1 = answer(hidden_1, grads_1, *weights, 1, ())
    ring_0.step()
    back_1 = exchange(gate(ret_1, *ring_1.now()))
    ring_0.step()
    shard_0 = ring_0.finish()
    sums_0 = unpack(pick[0], back_0, 0, ())
    ring_1.step()
    ring_1.step(sums_0)
    ring_1.step()
    shard_1 = ring_1.finish()
    layer_out, grad_tokens = unpack(pick[1], back_1, 1, sums_0)
    shards = jnp.stack([shard_0, shard_1])
    return (
        layer_out,
        grad_tokens,
        shards[:, :GATE_ROWS, :HID],
        shards[:, :GATE_ROWS, HID:],
        shards[:, GATE_ROWS:, :],
    )


def solution(mesh):
    return jax.shard_map(
        per_device,
        mesh=mesh,
        in_specs=(
            P(("dp", "expert"), None),
            P(("dp", "expert"), None),
            P(("dp", "expert")),
            P(("dp", "expert"), None),
            P("expert", None, None),
            P("expert", None, None),
            P("expert", None, None),
        ),
        out_specs=(
            P(("dp", "expert"), None),
            P(("dp", "expert"), None),
            P("expert", "dp", None),
            P("expert", "dp", None),
            P("expert", "dp", None),
        ),
        check_vma=False,
    )
```

```python
import functools

import jax
import jax.numpy as jnp
from jax import lax
from jax.experimental import pallas as pl
from jax.experimental.pallas import tpu as pltpu
from jax.sharding import PartitionSpec as P

D = 1024
HID = 512
TOK = 256
CAP = 40
GROUPS = 16
CHUNKS = 2
ROWS = GROUPS * CAP
RING = 8
HI = 2
GATE_ROWS = D // RING // HI
DOWN_ROWS = HID // RING // HI
SHARD_ROWS = GATE_ROWS + DOWN_ROWS
VMEM = pl.BlockSpec(memory_space=pltpu.VMEM)
ANY = pl.BlockSpec(memory_space=pl.ANY)
SMEM = pl.BlockSpec(memory_space=pltpu.SMEM)
BF16 = jnp.bfloat16
F32 = jnp.float32


def mm(a, b, dims=((1,), (0,))):
    return lax.dot_general(a, b, (dims, ((), ())), preferred_element_type=F32)


def whole(*shape):
    return pl.BlockSpec(shape, lambda i: (0,) * len(shape))


def one(chunk, *shape):
    return pl.BlockSpec((1,) + shape, lambda i: (chunk, 0, 0))


def slot_rows(ids_ref, quant_ref, chunk):
    first, second = ids_ref[0:1, :], ids_ref[1:2, :]
    expert = lax.broadcasted_iota(jnp.int32, (GROUPS, TOK), 0) * CHUNKS + chunk
    is_first = expert == first
    chosen = is_first | (expert == second)
    before = lax.broadcasted_iota(jnp.int32, (TOK, TOK), 0) < lax.broadcasted_iota(
        jnp.int32, (TOK, TOK), 1
    )
    rank = mm(
        jnp.where(chosen, 1.0, 0.0).astype(BF16), jnp.where(before, 1.0, 0.0).astype(BF16)
    )
    place = jnp.where(chosen, rank.astype(jnp.int32), -1)
    share = quant_ref[...].astype(F32) / 256.0
    share = jnp.where(is_first, share, 1.0 - share)
    row = lax.broadcasted_iota(jnp.int32, (CAP, TOK), 0)
    hit = [row == place[g : g + 1, :] for g in range(GROUPS)]
    plain = jnp.concatenate([jnp.where(h, 1.0, 0.0) for h in hit], axis=0)
    weighted = jnp.concatenate(
        [jnp.where(h, share[g : g + 1, :], 0.0) for g, h in enumerate(hit)], axis=0
    )
    return plain.astype(BF16), weighted.astype(BF16)


def pack_kernel(chunk, ids_ref, quant_ref, tokens_ref, cot_ref, *refs):
    send_ref, plain_ref, weighted_ref = refs[-3:]

    @pl.when(pl.program_id(0) == 0)
    def _():
        plain_ref[...], weighted_ref[...] = slot_rows(ids_ref, quant_ref, chunk)

    width = tokens_ref.shape[1]
    rows = mm(plain_ref[...], tokens_ref[...])
    send_ref[:, 0] = rows.reshape(GROUPS, CAP, width).astype(BF16)
    rows = mm(weighted_ref[...], cot_ref[...])
    send_ref[:, 1] = rows.reshape(GROUPS, CAP, width).astype(BF16)


def pack(ids, quant, tokens, cotangent, chunk, after):
    steps = 4
    columns = pl.BlockSpec((TOK, D // steps), lambda i: (0, i))
    return pl.pallas_call(
        functools.partial(pack_kernel, chunk),
        grid=(steps,),
        out_shape=pltpu.HBM((GROUPS, 2, CAP, D), BF16),
        in_specs=[whole(2, TOK), whole(1, TOK), columns, columns] + [ANY] * len(after),
        out_specs=pl.BlockSpec((GROUPS, 2, CAP, D // steps), lambda i: (0, 0, 0, i)),
        scratch_shapes=[pltpu.VMEM((ROWS, TOK), BF16)] * 2,
        compiler_params=pltpu.CompilerParams(vmem_limit_bytes=(60 if chunk == 0 else 24) << 20),
        cost_estimate=pl.CostEstimate(
            flops=4 * ROWS * TOK * D, bytes_accessed=4 << 20, transcendentals=0
        ),
        name=f"pack_{chunk}",
    )(ids, quant, tokens, cotangent, *after)


def pick_kernel(ids_ref, quant_ref, *pick_refs):
    for chunk, pick_ref in enumerate(pick_refs):
        for kind, rows in enumerate(slot_rows(ids_ref, quant_ref, chunk)):
            pick_ref[kind] = rows.astype(F32).T.astype(BF16)


def picks(ids, quant):
    return pl.pallas_call(
        pick_kernel,
        grid=(1,),
        out_shape=[pltpu.HBM((2, TOK, ROWS), BF16)] * CHUNKS,
        in_specs=[whole(2, TOK), whole(1, TOK)],
        out_specs=[whole(2, TOK, ROWS)] * CHUNKS,
        compiler_params=pltpu.CompilerParams(vmem_limit_bytes=20 << 20),
        cost_estimate=pl.CostEstimate(
            flops=4 * TOK * TOK * GROUPS, bytes_accessed=2 << 20, transcendentals=0
        ),
        name="picks",
    )(ids, quant)


def expert_kernel(chunk, waits, z_ref, recv_ref, gate_ref, up_ref, down_ref, *refs):
    hidden_ref, grads_ref, *refs = refs[waits:]
    part_refs, (grad_gu, grad_down, *held, sems) = refs[:RING], refs[RING:]
    recv, w_gate, w_up, w_down = held
    sources = (recv_ref, gate_ref.at[chunk], up_ref.at[chunk], down_ref.at[chunk])
    loads = [
        pltpu.make_async_copy(source, to, sems.at[i])
        for i, (source, to) in enumerate(zip(sources, held))
    ]
    for load in loads:
        load.start()
    loads[0].wait()
    rows = recv[:, 0].astype(F32).reshape(ROWS, D).astype(BF16)
    routed = recv[:, 1].astype(F32).reshape(ROWS, D).astype(BF16)
    loads[1].wait()
    gate_value = mm(rows, w_gate[...])
    loads[2].wait()
    up_value = mm(rows, w_up[...])
    sig = jax.nn.sigmoid(gate_value)
    act = gate_value * sig
    hidden = (act * up_value).astype(BF16)
    loads[3].wait()
    hidden_grad = mm(routed, w_down[...], ((1,), (1,)))
    gate_grad = (hidden_grad * up_value * sig * (1.0 + gate_value * (1.0 - sig))).astype(BF16)
    up_grad = (hidden_grad * act).astype(BF16)
    both = jnp.concatenate([gate_grad, up_grad], axis=1)
    hidden_ref[...] = hidden
    grads_ref[...] = both
    grad_gu[...] = mm(rows, both, ((0,), (0,)))
    grad_down[...] = mm(hidden, routed, ((0,), (0,)))
    z = z_ref[0]
    for j, part_ref in enumerate(part_refs):
        owner = lax.rem(z + j, RING)
        for h in range(HI):
            at = pl.multiple_of((owner * HI + h) * GATE_ROWS, GATE_ROWS)
            part_ref[h, :GATE_ROWS] = grad_gu[pl.ds(at, GATE_ROWS), :].astype(BF16)
            at = pl.multiple_of((owner * HI + h) * DOWN_ROWS, DOWN_ROWS)
            part_ref[h, GATE_ROWS:] = grad_down[pl.ds(at, DOWN_ROWS), :].astype(BF16)


def held_in(space, *arrays):
    return [pltpu.with_memory_space_constraint(a, space) for a in arrays]


def expert(z, recv, w_gate, w_up, w_down, chunk, after):
    part = pltpu.VMEM((HI, SHARD_ROWS, D), BF16)
    weight = 3 if chunk else 1
    hidden, grads, *parts = pl.pallas_call(
        functools.partial(expert_kernel, chunk, len(after)),
        out_shape=[pltpu.VMEM((ROWS, HID), BF16), pltpu.VMEM((ROWS, 2 * HID), BF16)]
        + [part] * RING,
        in_specs=[SMEM] + [ANY] * (4 + len(after)),
        out_specs=[VMEM] * (2 + RING),
        scratch_shapes=[pltpu.VMEM((D, 2 * HID), F32), pltpu.VMEM((HID, D), F32)]
        + [pltpu.VMEM((GROUPS, 2, CAP, D), BF16)]
        + [pltpu.VMEM((D, HID), BF16)] * 2
        + [pltpu.VMEM((HID, D), BF16), pltpu.SemaphoreType.DMA((4,))],
        compiler_params=pltpu.CompilerParams(vmem_limit_bytes=27 << 20),
        cost_estimate=pl.CostEstimate(
            flops=weight * 12 * ROWS * D * HID,
            bytes_accessed=weight * 10 << 20,
            transcendentals=ROWS * HID,
        ),
        name=f"expert_{chunk}",
    )(z, *held_in(pltpu.HBM, recv, w_gate, w_up, w_down), *after)
    return hidden, grads, parts


def answer_kernel(hidden_ref, grads_ref, gate_ref, up_ref, down_ref, *refs):
    ret_ref, token_ref = refs[-2:]
    token_ref[...] = jnp.zeros_like(token_ref)
    groups = ret_ref.shape[0]
    out = mm(hidden_ref[...], down_ref[0])
    ret_ref[:, 0] = out.reshape(groups, CAP, D).astype(BF16)
    input_grad = mm(grads_ref[:, :HID], gate_ref[0], ((1,), (1,)))
    input_grad += mm(grads_ref[:, HID:], up_ref[0], ((1,), (1,)))
    ret_ref[:, 1] = input_grad.reshape(groups, CAP, D).astype(BF16)


def answer(hidden, grads, w_gate, w_up, w_down, chunk, after):
    steps = 2
    return pl.pallas_call(
        answer_kernel,
        grid=(steps,),
        out_shape=[pltpu.HBM((GROUPS, 2, CAP, D), BF16), jax.ShapeDtypeStruct((8, 128), F32)],
        in_specs=[
            pl.BlockSpec((ROWS // steps, HID), lambda i: (i, 0)),
            pl.BlockSpec((ROWS // steps, 2 * HID), lambda i: (i, 0)),
        ]
        + [one(chunk, D, HID), one(chunk, D, HID), one(chunk, HID, D)]
        + [ANY] * len(after),
        out_specs=[
            pl.BlockSpec((GROUPS // steps, 2, CAP, D), lambda i: (i, 0, 0, 0)),
            whole(8, 128),
        ],
        compiler_params=pltpu.CompilerParams(vmem_limit_bytes=24 << 20),
        cost_estimate=pl.CostEstimate(
            flops=6 * ROWS * D * HID, bytes_accessed=8 << 20, transcendentals=0
        ),
        name=f"answer_{chunk}",
    )(hidden, grads, *held_in(pltpu.HBM, w_gate, w_up, w_down), *after)


def unpack_kernel(pick_ref, ret_ref, *refs):
    *earlier, layer_ref, grad_ref = refs
    width = layer_ref.shape[1]
    for kind, out_ref in ((0, layer_ref), (1, grad_ref)):
        rows = ret_ref[:, kind].astype(F32).reshape(ROWS, width).astype(BF16)
        total = mm(pick_ref[1 - kind], rows)
        if earlier:
            total += earlier[kind][...]
        out_ref[...] = total.astype(out_ref.dtype)


def unpack(pick, returned, chunk, earlier):
    steps = 2
    columns = pl.BlockSpec((TOK, D // steps), lambda i: (0, i))
    last = chunk == CHUNKS - 1
    return pl.pallas_call(
        unpack_kernel,
        grid=(steps,),
        out_shape=[jax.ShapeDtypeStruct((TOK, D), BF16 if last else F32)] * 2,
        in_specs=[
            whole(2, TOK, ROWS),
            pl.BlockSpec((GROUPS, 2, CAP, D // steps), lambda i: (0, 0, 0, i)),
        ]
        + [columns] * len(earlier),
        out_specs=[columns] * 2,
        compiler_params=pltpu.CompilerParams(vmem_limit_bytes=20 << 20),
        cost_estimate=pl.CostEstimate(
            flops=4 * ROWS * TOK * D, bytes_accessed=4 << 20, transcendentals=0
        ),
        name=f"unpack_{chunk}",
    )(*held_in(pltpu.HBM, pick, returned), *earlier)


def nothing(*refs):
    pass


def gate(array, *after):
    return pl.pallas_call(
        nothing,
        out_shape=pltpu.HBM(array.shape, array.dtype),
        in_specs=[ANY] * (1 + len(after)),
        out_specs=pl.BlockSpec(memory_space=pltpu.HBM),
        input_output_aliases={0: 0},
        cost_estimate=pl.CostEstimate(flops=0, bytes_accessed=0, transcendentals=0),
        name="gate",
    )(*held_in(pltpu.HBM, array), *after)


def ring_step(held, sign, across=0):
    step = [
        (i, (i // HI + sign) % RING * HI + (i + across) % HI) for i in range(RING * HI)
    ]
    return lax.ppermute(held, "dp", step)


def add_part(held, part):
    return (held.astype(F32) + part.astype(F32)).astype(BF16)


class Ring:
    def __init__(self, parts, up_hops):
        self.parts = parts
        self.hops = {1: up_hops, -1: RING - 1 - up_hops}
        self.held = {s: parts[s * n % RING] for s, n in self.hops.items()}

    def step(self, up=(), down=()):
        for sign, left in self.hops.items():
            if left:
                self.hops[sign] = left - 1
                held = ring_step(self.held[sign], sign)
                if left > 1:
                    part, *_ = lax.optimization_barrier(
                        (self.parts[sign * (left - 1) % RING], *(up if sign > 0 else down))
                    )
                    held = add_part(held, part)
                self.held[sign] = held

    def now(self):
        return self.held[1], self.held[-1]

    def before(self, *others):
        up, down, *others = lax.optimization_barrier((self.held[1], self.held[-1], *others))
        self.held = {1: up, -1: down}
        return others

    def finish(self):
        total = (
            self.parts[0].astype(F32) + self.held[1].astype(F32) + self.held[-1].astype(F32)
        )
        mine, other = halves(total)
        return mine + ring_step(other.astype(BF16), 0, 1).astype(F32)

    def finish_direct(self, sign):
        total = self.parts[0].astype(F32) + self.held[-sign].astype(F32)
        mine, other = halves(total)
        same, cross = halves(self.held[sign])
        arrived = [
            ring_step(same, sign),
            ring_step(cross, sign, 1),
            ring_step(other.astype(BF16), 0, 1),
        ]
        return mine + sum(a.astype(F32) for a in arrived)


def halves(pair):
    hi = lax.axis_index("dp") % HI
    return [lax.dynamic_index_in_dim(pair, h, 0, keepdims=False) for h in (hi, 1 - hi)]


def exchange(rows):
    return lax.all_to_all(rows, "expert", 0, 0, tiled=True)


def per_device(tokens, expert_ids, gate_quant, cotangent, w_gate, w_up, w_down):
    ids, quant = expert_ids.T, gate_quant[None, :]
    weights = (w_gate, w_up, w_down)
    z = (lax.axis_index("dp") // HI).astype(jnp.int32).reshape(1)
    pick = picks(ids, quant)
    recv_0 = exchange(pack(ids, quant, tokens, cotangent, 0, ()))
    recv_1 = exchange(pack(ids, quant, tokens, cotangent, 1, pick))
    hidden_0, grads_0, parts_0 = expert(z, recv_0, *weights, 0, ())
    ring_0 = Ring(parts_0, 3)
    ret_0, _ = answer(hidden_0, grads_0, *weights, 0, ())
    ring_0.step()
    back_0 = exchange(gate(ret_0, *ring_0.now()))
    ring_0.step()
    hidden_1, grads_1, parts_1 = expert(z, recv_1, *weights, 1, ring_0.now())
    ring_1 = Ring(parts_1, 4)
    ret_1, token = answer(hidden_1, grads_1, *weights, 1, ())
    ring_1.step((token,), (token,))
    ring_0.step()
    back_1 = exchange(gate(ret_1, *ring_1.now()))
    ring_0.step()
    shard_0 = ring_0.finish()
    sums_0 = unpack(pick[0], back_0, 0, ())
    ring_1.step()
    ring_1.step(sums_0)
    ring_1.step()
    shard_1 = ring_1.finish()
    layer_out, grad_tokens = unpack(pick[1], back_1, 1, sums_0)
    shards = jnp.stack([shard_0, shard_1])
    return (
        layer_out,
        grad_tokens,
        shards[:, :GATE_ROWS, :HID],
        shards[:, :GATE_ROWS, HID:],
        shards[:, GATE_ROWS:, :],
    )


def solution(mesh):
    return jax.shard_map(
        per_device,
        mesh=mesh,
        in_specs=(
            P(("dp", "expert"), None),
            P(("dp", "expert"), None),
            P(("dp", "expert")),
            P(("dp", "expert"), None),
            P("expert", None, None),
            P("expert", None, None),
            P("expert", None, None),
        ),
        out_specs=(
            P(("dp", "expert"), None),
            P(("dp", "expert"), None),
            P("expert", "dp", None),
            P("expert", "dp", None),
            P("expert", "dp", None),
        ),
        check_vma=False,
    )
```
